32 devices in a mesh: grp: 2 (over x), ex: 4 (over y, core), at: 4 (over z).
Axes of the slice: x: 2, y: 2, z: 4, core: 2. Of those that a mesh axis runs over, the one named last changes fastest.
Arguments:
- tokens: bfloat16 [256, 7168], P(('grp', 'ex', 'at')), parts along dimension 0, may hold values from -6 to 6
- expert_ids: int32 [256, 8], P(('grp', 'ex', 'at')), parts along dimension 0, may hold values from 0 to 15, all different within a row; in each aligned block of 8 rows (0 to 7, 8 to 15, ...) at most 5 rows name the same one
- gates: bfloat16 [256, 8], P(('grp', 'ex', 'at')), parts along dimension 0, may hold values from 0.099609375 to 0.59765625
- w_in: bfloat16 [16, 7168, 2, 2048], P('ex', None, None, 'at'), may hold values from -0.0625 to 0.0625
- w_out: bfloat16 [16, 2048, 7168], P('ex', 'at'), may hold values from -0.125 to 0.125
- q_latent: bfloat16 [128, 64, 512], P(('grp', 'ex', 'at')), parts along dimension 0, may hold values from -8 to 8
- q_rope: bfloat16 [128, 4096], P(('grp', 'ex', 'at')), parts along dimension 0, may hold values from -8 to 8
- cache_latent: bfloat16 [128, 256, 512], P(('grp', 'ex', 'at')), parts along dimension 0, may hold values from -4 to 4
- cache_rope: bfloat16 [128, 64, 256], P(('grp', 'ex', 'at')), parts along dimension 0, may hold values from -4 to 4
- lengths: int32 [128], P(('grp', 'ex', 'at')), parts along dimension 0, may hold values from 2 to 256, as said below
Outputs:
- moe_out: bfloat16 [256, 7168], P(('grp', 'ex', 'at')), parts along dimension 0
- context: bfloat16 [128, 64, 512], P(('grp', 'ex', 'at')), parts along dimension 0
The draws below stay inside these ranges and needn't reach their ends.
There are 2 independent parts, one for each index of `grp`. The reference program is written for one: setup_inputs(seed, part) draws one part's arguments, and reference() takes and returns one part's arrays. A program takes and returns all parts, laid end to end along the dimension named above; an argument that names none is the same for every part. Nothing has to cross between parts.
Inputs may be any that keep to these rules, and one draw needn't show every extreme that they name: `expert_ids`: A row's 8 ids differ. In each aligned block of 8 rows (the rows of one device) no expert is named by more than 5 rows, and in every draw some block has an expert named by exactly 5 rows. `lengths`: in each aligned block of 4 sequences (those of one device) one sequence has 256 positions.
All inputs are finite; a program needn't handle non-finite values.
Results may differ from the reference program's by a relative error of at most 0.0085.
Values may be sent and summed in bfloat16 or wider, within the bound.
A program may use at most 320 MiB of HBM per device.

```python
import math
import jax
import jax.numpy as jnp
import numpy as np
from jax import lax

D = 7168
FF = 2048
LATENT = 512
ROPE = 64
TOP = 8
HEADS = 64
TOK_DEV = 8
CAP = 5
ATT_DEV = 4
CTX = 256
EXPERTS = 16
TOKENS = 128
ATT_ROWS = 64
N_EX = 4
N_AT = 4


def draw_q_latent(key, part):
    key = jax.random.fold_in(key, 1)
    normal_part = jax.random.truncated_normal(key, -4.0, 4.0, (ATT_ROWS, HEADS, LATENT), jnp.float32)
    return normal_part.astype(jnp.bfloat16)


def draw_q_rope(key, part):
    key = jax.random.fold_in(key, 2)
    normal_part = jax.random.truncated_normal(key, -4.0, 4.0, (ATT_ROWS, HEADS * ROPE), jnp.float32)
    return normal_part.astype(jnp.bfloat16)


def draw_cache_latent(key, part):
    key = jax.random.fold_in(key, 3)
    normal_part = jax.random.truncated_normal(key, -4.0, 4.0, (ATT_ROWS, CTX, LATENT), jnp.float32)
    return normal_part.astype(jnp.bfloat16)


def draw_cache_rope(key, part):
    key = jax.random.fold_in(key, 4)
    normal_part = jax.random.truncated_normal(key, -4.0, 4.0, (ATT_ROWS, ROPE, CTX), jnp.float32)
    return normal_part.astype(jnp.bfloat16)


def draw_lengths(key, part):
    key = jax.random.fold_in(key, 5)
    uniform_draw = jax.random.randint(jax.random.fold_in(key, 1), (ATT_ROWS,), 0, CTX - 1)
    factor = jax.random.randint(jax.random.fold_in(key, 2), (ATT_ROWS // ATT_DEV,), 1, 5)
    ragged = 2 + uniform_draw * jnp.repeat(factor, ATT_DEV) // 4
    full_pick = jax.random.randint(jax.random.fold_in(key, 3), (ATT_ROWS // ATT_DEV,), 0, ATT_DEV)
    is_full = jnp.arange(ATT_ROWS) % ATT_DEV == jnp.repeat(full_pick, ATT_DEV)
    return jnp.where(is_full, CTX, ragged).astype(jnp.int32)


def level_of(own_key, shape, shards, low, high):
    factor_of = 1.0
    for axis_at, blocks in shards:
        steps = jax.random.uniform(jax.random.fold_in(jax.random.fold_in(own_key, 6), axis_at), (blocks,), jnp.float32, low / len(shards), high / len(shards))
        factor_of = factor_of * jnp.repeat(jnp.exp(steps), shape[axis_at] // blocks).reshape((-1,) + (1,) * (len(shape) - 1 - axis_at))
    return factor_of


def routed_block(key, own, number, rows, amount, top, most, skew):
    sequence = jax.random.permutation(key, amount)
    heavy_load, ordinary = portions_of(amount, rows * top, most, skew, True), portions_of(amount, rows * top, most, skew, False)
    places = jnp.arange(amount)

    def named(tallies, turn):
        used = int((tallies > 0).sum())
        fixed = max(1, used // 4)
        shifted = fixed + (places - fixed + turn * (used - fixed)) % max(1, amount - fixed)
        return jnp.zeros((amount,), jnp.int32).at[sequence[jnp.where(places < fixed, places, shifted)]].set(jnp.asarray(tallies, jnp.int32))

    tallies = jnp.where(number % 4 == 0, named(heavy_load, number // 4), named(ordinary, number - number // 4 - 1))
    mixed = jax.random.permutation(jax.random.fold_in(own, 3), amount)
    donor, taker = mixed[0:amount // 2 * 2:2], mixed[1:amount // 2 * 2:2]
    margin = jnp.minimum(tallies[donor] - 1, most - tallies[taker]) // 2
    margin = jnp.where((donor == sequence[0]) | (taker == sequence[0]) | (tallies[taker] == 0), 0, jnp.maximum(margin, 0))
    shifted = jax.random.randint(jax.random.fold_in(own, 4), (amount // 2,), 0, 1 << 20) % (margin + 1)
    tallies = tallies.at[donor].add(-shifted).at[taker].add(shifted)
    labels = jnp.searchsorted(jnp.cumsum(tallies), jnp.arange(rows * top), side="right").astype(jnp.int32)
    listing = labels.reshape(top, rows).T
    listing = listing[jax.random.permutation(jax.random.fold_in(own, 1), rows)]
    turn = jax.random.randint(jax.random.fold_in(own, 2), (rows, 1), 0, top)
    return jnp.take_along_axis(listing, (jnp.arange(top)[None, :] + turn) % top, axis=1)


def portions_of(amount, total, most, skew, full):
    weights = [(1 << 20) // math.isqrt(grade ** skew) + 1 for grade in range(1, amount + 1)]
    largest = most if full else min(most, max(-(-total // amount), total * weights[0] // sum(weights)))
    least = 1 if total - largest >= amount - 1 else 0
    counts, spare = [largest] + [least] * (amount - 1), total - largest - least * (amount - 1)
    while spare > 0:
        candidates = [i for i in range(1, amount) if counts[i] < largest] or [i for i in range(1, amount) if counts[i] < most]
        mass, budget = sum([weights[i] for i in candidates]), spare
        for i in candidates:
            extra = min(most - counts[i], max(1, budget * weights[i] // mass), spare)
            counts[i] = counts[i] + extra
            spare = spare - extra
    return np.array(counts)


def noise(key, extent, scale, bound, split=(), held_as=jnp.bfloat16):
    array = scale * jax.random.normal(key, extent, jnp.float32)
    if split:
        array = array * level_of(key, extent, split, -0.22, 0.18)
    return jnp.clip(array, -bound, bound).astype(held_as)


def setup_inputs(seed: int = 0, part: int = 0) -> dict:
    key_list = jax.random.split(jax.random.key(seed), 11)
    part_splits = jax.random.split(jax.random.fold_in(key_list[10], part), 11)
    tokens = noise(part_splits[0], (TOKENS, D), 1.0, 6.0, ((0, 16),))
    expert_ids_keys = jax.random.split(jax.random.fold_in(part_splits[1], 1), TOKENS // TOK_DEV)
    expert_ids_turns = jax.random.permutation(jax.random.fold_in(part_splits[1], 3), TOKENS // TOK_DEV)
    expert_ids = jax.vmap(lambda own, number: routed_block(jax.random.fold_in(part_splits[1], 2), own, number, TOK_DEV, EXPERTS, TOP, CAP, 2))(expert_ids_keys, expert_ids_turns).reshape((TOKENS, TOP))
    gates = jnp.clip(0.099609375 + 0.49804688 * jax.random.uniform(part_splits[2], (TOKENS, TOP), jnp.float32) ** level_of(part_splits[2], (TOKENS, TOP), ((0, 16),), -0.2, 0.2), 0.099609375, 0.59765625).astype(jnp.bfloat16)
    w_in = noise(key_list[3], (EXPERTS, D, 2, FF), D ** -0.5, 0.0625, ((0, 4), (3, 4)))
    w_out = noise(key_list[4], (EXPERTS, FF, D), FF ** -0.5, 0.125, ((0, 4), (1, 4)))
    q_latent = draw_q_latent(jax.random.fold_in(jax.random.fold_in(key_list[10], part), 71), part)
    q_rope = draw_q_rope(jax.random.fold_in(jax.random.fold_in(key_list[10], part), 71), part)
    cache_latent = draw_cache_latent(jax.random.fold_in(jax.random.fold_in(key_list[10], part), 71), part)
    cache_rope = draw_cache_rope(jax.random.fold_in(jax.random.fold_in(key_list[10], part), 71), part)
    lengths = draw_lengths(jax.random.fold_in(jax.random.fold_in(key_list[10], part), 71), part)
    return dict(tokens=tokens, expert_ids=expert_ids, gates=gates, w_in=w_in, w_out=w_out, q_latent=q_latent, q_rope=q_rope, cache_latent=cache_latent, cache_rope=cache_rope, lengths=lengths)


def expert_layer(tokens, expert_ids, gates, w_in, w_out):
    flat_ids = expert_ids.reshape(-1)
    owner_row = (jnp.arange(TOKENS * TOP) // TOP).astype(jnp.int32)
    flat_gates = gates.reshape(-1).astype(jnp.float32)
    max_rows = N_EX * N_AT * CAP
    hid_units = FF // N_AT

    def one_expert(running, expert):
        chosen = flat_ids == expert
        ordering = jnp.argsort(jnp.where(chosen, 0, 1).astype(jnp.int32), stable=True)[:max_rows]
        is_valid = chosen[ordering]
        owners = owner_row[ordering]
        row_block = tokens[owners]
        gate_up = jnp.dot(row_block, w_in[expert].reshape(D, 2 * FF), preferred_element_type=jnp.float32)
        hidden = (jax.nn.silu(gate_up[:, :FF]) * gate_up[:, FF:]).astype(jnp.bfloat16)
        down_out = jnp.einsum('rbh,bhd->rbd', hidden.reshape(max_rows, N_AT, hid_units).astype(jnp.float32),
                              w_out[expert].reshape(N_AT, hid_units, D).astype(jnp.float32))
        gate_col = jnp.where(is_valid, flat_gates[ordering], jnp.float32(0.0))
        partial_value = (down_out * gate_col[:, None, None]).astype(jnp.bfloat16)
        partial_value = lax.optimization_barrier(partial_value).astype(jnp.float32).sum(axis=1)
        return running.at[owners].add(partial_value), None

    start_out = jnp.zeros((TOKENS, D), jnp.float32)
    summed, _ = lax.scan(one_expert, start_out, jnp.arange(EXPERTS, dtype=jnp.int32))
    return summed.astype(jnp.bfloat16)


def latent_attention(q_latent, q_rope, cache_latent, cache_rope, lengths):
    rope_q = q_rope.reshape(ATT_ROWS, HEADS, ROPE).astype(jnp.float32)
    scores = jnp.einsum('ahl,acl->ahc', q_latent.astype(jnp.float32), cache_latent.astype(jnp.float32))
    scores = scores + jnp.einsum('ahr,arc->ahc', rope_q, cache_rope.astype(jnp.float32))
    scores = scores * (192.0 ** -0.5)
    visible = jnp.arange(CTX)[None, None, :] < lengths[:, None, None]
    scores = jnp.where(visible, scores, -1e30)
    peak = jnp.max(scores, axis=2, keepdims=True)
    expo = jnp.where(visible, jnp.exp(scores - peak), 0.0)
    probs = (expo / jnp.sum(expo, axis=2, keepdims=True)).astype(jnp.bfloat16)
    context = jnp.einsum('ahc,acl->ahl', probs.astype(jnp.float32), cache_latent.astype(jnp.float32))
    return context.astype(jnp.bfloat16)


def reference(tokens, expert_ids, gates, w_in, w_out, q_latent, q_rope, cache_latent, cache_rope, lengths):
    moe_out = expert_layer(tokens, expert_ids, gates, w_in, w_out)
    context = latent_attention(q_latent, q_rope, cache_latent, cache_rope, lengths)
    return (moe_out, context)
```

```python
import functools

import jax
import jax.numpy as jnp
from jax import lax
from jax.experimental import pallas as pl
from jax.experimental.pallas import tpu as pltpu
from jax.sharding import PartitionSpec as P

CAP = 5
LANES = 128
D_BLOCK = 1024
W_SLOTS = 12
O_COLS = 512
O_SLOTS = 6


def moe_kernel(
    x_ref, win_ref, wout_ref, o_ref,
    xg, xe, wbuf, obuf, acc, hid, keep1, out1, in1, keep2, out2, in2, keep3, out3, in3,
    wsem, osem, zs, zr, ys, yr, cs, cr, s1, q1, s2, q2, s3, q3,
):
    experts_here, model_width, jbs = win_ref.shape[:3]
    hid_units = wout_ref.shape[1]
    at_count = 4
    tok_rows = x_ref.shape[0]
    rows = 16 * tok_rows
    e0 = lax.axis_index("ex")
    a0 = lax.axis_index("at")
    y0 = e0 // 2
    c0 = e0 % 2
    e_y = (1 - y0) * 2 + c0
    e_c = y0 * 2 + (1 - c0)
    d_chunks = model_width // D_BLOCK
    w_chunks = experts_here * d_chunks
    o_chunks = model_width // O_COLS

    def w_copy(i, jb):
        return pltpu.make_async_copy(
            win_ref.at[i // d_chunks, pl.ds((i % d_chunks) * D_BLOCK, D_BLOCK), jb],
            wbuf.at[i % W_SLOTS, jb],
            wsem.at[i % W_SLOTS, jb],
        )

    def o_copy(i):
        return pltpu.make_async_copy(
            wout_ref.at[:, :, pl.ds(pl.multiple_of(i * O_COLS, O_COLS), O_COLS)],
            obuf.at[i % O_SLOTS],
            osem.at[i % O_SLOTS],
        )

    def w_start(i, carry):
        for jb in range(jbs):
            w_copy(i, jb).start()
        return carry

    def o_start(i, carry):
        o_copy(i).start()
        return carry

    lax.fori_loop(0, W_SLOTS, w_start, 0)

    to_z = [{"ex": e0, "at": (a0 + j) % at_count} for j in range(at_count)]
    to_y = {"ex": e_y, "at": a0}
    to_c = {"ex": e_c, "at": a0}
    barrier = pltpu.get_barrier_semaphore()
    for peer in to_z[1:] + [to_y, to_c]:
        pl.semaphore_signal(barrier, inc=1, device_id=peer, device_id_type=pl.DeviceIdType.MESH)
    pl.semaphore_wait(barrier, at_count + 1)

    def remote(src, dst, send, recv, peer):
        return pltpu.make_async_remote_copy(
            src_ref=src, dst_ref=dst, send_sem=send, recv_sem=recv,
            device_id=peer, device_id_type=pl.DeviceIdType.MESH,
        )

    def block(ex, j):
        return ex * at_count + (a0 + at_count - j) % at_count

    def z_copy(j, slot):
        return remote(xg.at[slot], xg.at[slot], zs.at[j - 1], zr.at[j - 1], to_z[j])

    def y_copy(j, slot):
        return remote(xg.at[slot], xg.at[slot], ys.at[j], yr.at[j], to_y)

    def c_copy(j, slot):
        return remote(xg.at[slot], xg.at[slot], cs.at[j], cr.at[j], to_c)

    own = block(e0, 0)
    xg[own] = x_ref[...]
    for j in range(1, at_count):
        z_copy(j, own).start()
    y_copy(0, own).start()
    c_copy(0, own).start()
    lax.fori_loop(0, O_SLOTS, o_start, 0)
    for j in (1, 3, 2):
        z_copy(j, block(e0, j)).wait_recv()
        y_copy(j, block(e0, j)).start()
        c_copy(j, block(e0, j)).start()
    for j in (0, 1, 3, 2):
        y_copy(j, block(e_y, j)).wait_recv()
        c_copy(4 + j, block(e_y, j)).start()
    for j in (0, 1, 3, 2):
        c_copy(j, block(e_c, j)).wait_recv()
    for j in (0, 1, 3, 2):
        c_copy(4 + j, block((1 - y0) * 2 + (1 - c0), j)).wait_recv()

    row = lax.broadcasted_iota(jnp.int32, (LANES, 2 * LANES), 0)
    col = lax.broadcasted_iota(jnp.int32, (LANES, 2 * LANES), 1)
    spread = [(col == 2 * row + p).astype(jnp.bfloat16) for p in range(2)]

    def expand(i, carry):
        x = xg[:, :, pl.ds(pl.multiple_of(i * LANES, LANES), LANES)].astype(jnp.float32)
        x = x.reshape(rows, LANES).astype(jnp.bfloat16)
        for p in range(2):
            xe[p * rows:(p + 1) * rows, pl.ds(pl.multiple_of(i * 2 * LANES, 2 * LANES), 2 * LANES)] = (
                jnp.dot(x, spread[p], preferred_element_type=jnp.float32).astype(jnp.bfloat16)
            )
        return carry

    lax.fori_loop(0, model_width // LANES, expand, 0)
    dense = xg[:, :, model_width:model_width + LANES].astype(jnp.float32).reshape(rows, LANES)
    lane = lax.broadcasted_iota(jnp.int32, (rows, LANES), 1)

    def one_expert(e, carry):
        acc[...] = jnp.zeros_like(acc)

        def step(d, inner):
            i = e * d_chunks + d
            for jb in range(jbs):
                w_copy(i, jb).wait()
            view = wbuf.at[i % W_SLOTS].reshape(jbs, 2 * D_BLOCK, LANES)
            x = xe[:, pl.ds(pl.multiple_of(d * 2 * D_BLOCK, 2 * D_BLOCK), 2 * D_BLOCK)]
            w = jnp.concatenate([view[jb] for jb in range(jbs)], axis=1)
            acc[...] += jnp.dot(x, w, preferred_element_type=jnp.float32)

            @pl.when(i + W_SLOTS < w_chunks)
            def _():
                w_start(i + W_SLOTS, 0)

            return inner

        lax.fori_loop(0, d_chunks, step, 0)
        gate = jnp.sum(jnp.where(lane == e0 * experts_here + e, dense, 0.0), axis=1, keepdims=True)
        hidden = jax.nn.silu(acc[:rows, :]) * acc[rows:, :] * gate
        hid[:, pl.ds(pl.multiple_of(e * hid_units, hid_units), hid_units)] = hidden.astype(jnp.bfloat16)
        return carry

    lax.fori_loop(0, experts_here, one_expert, 0)

    def core_copy(i):
        return remote(out1.at[i], in1.at[i], s1.at[i], q1.at[i], to_c)

    def row_copy(i):
        return remote(out2.at[i], in2.at[i], s2.at[i], q2.at[i], to_y)

    def col_copy(i, j):
        return remote(
            out3.at[i, (a0 + j) % at_count], in3.at[i, j - 1], s3.at[i, j - 1], q3.at[i, j - 1], to_z[j]
        )

    def down(i, carry):
        @pl.when(i < o_chunks)
        def _():
            o_copy(i).wait()
            w = obuf[i % O_SLOTS].reshape(experts_here * hid_units, O_COLS)
            part = jnp.dot(hid[...], w, preferred_element_type=jnp.float32)
            part = part.reshape(2, 2, rows // 4, O_COLS)
            keep1[i] = jnp.where(c0 == 0, part[:, 0], part[:, 1])
            out1[i] = jnp.where(c0 == 0, part[:, 1], part[:, 0]).astype(jnp.bfloat16)
            core_copy(i).start()

            @pl.when(i + O_SLOTS < o_chunks)
            def _():
                o_start(i + O_SLOTS, 0)

        @pl.when((i >= 1) & (i < o_chunks + 1))
        def _():
            k = i - 1
            core_copy(k).wait_recv()
            total = keep1[k] + in1[k].astype(jnp.float32)
            keep2[k] = jnp.where(y0 == 0, total[0], total[1])
            out2[k] = jnp.where(y0 == 0, total[1], total[0]).astype(jnp.bfloat16)
            row_copy(k).start()

        @pl.when((i >= 3) & (i < o_chunks + 3))
        def _():
            k = i - 3
            row_copy(k).wait_recv()
            total = keep2[k] + in2[k].astype(jnp.float32)
            total = total.reshape(at_count, tok_rows, O_COLS)
            out3[k] = total.astype(jnp.bfloat16)
            which = lax.broadcasted_iota(jnp.int32, total.shape, 0)
            keep3[k] = jnp.sum(jnp.where(which == a0, total, 0.0), axis=0)
            for j in range(1, at_count):
                col_copy(k, j).start()

        @pl.when(i >= 5)
        def _():
            k = i - 5
            for j in range(1, at_count):
                col_copy(k, j).wait_recv()
            total = keep3[k] + jnp.sum(in3[k].astype(jnp.float32), axis=0)
            o_ref[:, pl.ds(pl.multiple_of(k * O_COLS, O_COLS), O_COLS)] = total.astype(jnp.bfloat16)
            core_copy(k).wait_send()
            row_copy(k).wait_send()
            for j in range(1, at_count):
                col_copy(k, j).wait_send()

        return carry

    lax.fori_loop(0, o_chunks + 5, down, 0)
    for j in range(1, at_count):
        z_copy(j, own).wait_send()
    for j in range(at_count):
        y_copy(j, block(e0, j)).wait_send()
        c_copy(j, block(e0, j)).wait_send()
        c_copy(4 + j, block(e_y, j)).wait_send()


def fused_experts(tokens, expert_ids, gates, w_in, w_out):
    tok_rows, model_width = tokens.shape
    slot_count, _, pair, hid_units = w_in.shape
    rows = 16 * tok_rows
    chunks = model_width // O_COLS
    jbs = hid_units // LANES
    hit = expert_ids[:, :, None] == jnp.arange(LANES)[None, None, :]
    dense = jnp.sum(jnp.where(hit, gates[:, :, None], jnp.bfloat16(0)), axis=1)
    block = jnp.concatenate([tokens, dense.astype(jnp.bfloat16)], axis=1)
    view = w_in.reshape(slot_count, model_width, pair, jbs, LANES).transpose(0, 1, 3, 2, 4)
    bf16, f32 = jnp.bfloat16, jnp.float32
    dma = pltpu.SemaphoreType.DMA
    return pl.pallas_call(
        moe_kernel,
        out_shape=jax.ShapeDtypeStruct((tok_rows, model_width), bf16),
        in_specs=[
            pl.BlockSpec(memory_space=pltpu.VMEM),
            pl.BlockSpec(memory_space=pl.ANY),
            pl.BlockSpec(memory_space=pl.ANY),
        ],
        out_specs=pl.BlockSpec(memory_space=pltpu.VMEM),
        scratch_shapes=[
            pltpu.VMEM((16, tok_rows, model_width + LANES), bf16),
            pltpu.VMEM((2 * rows, 2 * model_width), bf16),
            pltpu.VMEM((W_SLOTS, jbs, D_BLOCK, 2, LANES), bf16),
            pltpu.VMEM((O_SLOTS, slot_count, hid_units, O_COLS), bf16),
            pltpu.VMEM((2 * rows, hid_units), f32),
            pltpu.VMEM((rows, slot_count * hid_units), bf16),
            pltpu.VMEM((chunks, 2, rows // 4, O_COLS), f32),
            pltpu.VMEM((chunks, 2, rows // 4, O_COLS), bf16),
            pltpu.VMEM((chunks, 2, rows // 4, O_COLS), bf16),
            pltpu.VMEM((chunks, rows // 4, O_COLS), f32),
            pltpu.VMEM((chunks, rows // 4, O_COLS), bf16),
            pltpu.VMEM((chunks, rows // 4, O_COLS), bf16),
            pltpu.VMEM((chunks, tok_rows, O_COLS), f32),
            pltpu.VMEM((chunks, 4, tok_rows, O_COLS), bf16),
            pltpu.VMEM((chunks, 3, tok_rows, O_COLS), bf16),
            dma((W_SLOTS, jbs)), dma((O_SLOTS,)),
            dma((3,)), dma((3,)), dma((4,)), dma((4,)), dma((8,)), dma((8,)),
            dma((chunks,)), dma((chunks,)), dma((chunks,)), dma((chunks,)),
            dma((chunks, 3)), dma((chunks, 3)),
        ],
        compiler_params=pltpu.CompilerParams(
            collective_id=0, has_side_effects=True, vmem_limit_bytes=61 << 20
        ),
    )(block, view, w_out)


def expert_part(row_block, row_gates, w_in, w_out):
    slot_count, model_width, pair_count, hid_units = w_in.shape
    gate_up = jnp.einsum(
        "srd,sdf->srf",
        row_block,
        w_in.reshape(slot_count, model_width, pair_count * hid_units),
        preferred_element_type=jnp.float32,
    )
    hidden = (jax.nn.silu(gate_up[..., :hid_units]) * gate_up[..., hid_units:]).astype(jnp.bfloat16)
    down_out = jnp.einsum("srf,sfd->srd", hidden, w_out, preferred_element_type=jnp.float32)
    return (down_out * row_gates[..., None].astype(jnp.float32)).astype(jnp.bfloat16)


def latent_attention(q_latent, q_rope, cache_latent, cache_rope, lengths):
    att_rows, head_count, latent_width = q_latent.shape
    positions = cache_latent.shape[1]
    rope_q = q_rope.reshape(att_rows, head_count, -1)
    scores = jnp.einsum("ahl,acl->ahc", q_latent, cache_latent, preferred_element_type=jnp.float32)
    scores = scores + jnp.einsum(
        "ahr,arc->ahc", rope_q, cache_rope, preferred_element_type=jnp.float32
    )
    scores = scores * 192.0 ** (-0.5)
    visible = jnp.arange(positions)[None, None, :] < lengths[:, None, None]
    scores = jnp.where(visible, scores, -1e30)
    peak = jnp.max(scores, axis=2, keepdims=True)
    expo = jnp.where(visible, jnp.exp(scores - peak), 0.0)
    probs = (expo / jnp.sum(expo, axis=2, keepdims=True)).astype(jnp.bfloat16)
    context = jnp.einsum("ahc,acl->ahl", probs, cache_latent, preferred_element_type=jnp.float32)
    return context.astype(jnp.bfloat16)


def routed_experts(
    tokens, expert_ids, gates, w_in, w_out
):
    tok_rows, model_width = tokens.shape
    top_count = expert_ids.shape[1]
    slot_count = w_in.shape[0]
    ex_count = lax.axis_size("ex")
    at_count = lax.axis_size("at")
    experts = slot_count * ex_count
    slot_rows = experts * CAP
    flat_ids = expert_ids.reshape(-1)
    onehot = (flat_ids[:, None] == jnp.arange(experts)[None, :]).astype(jnp.int32)
    before = jnp.cumsum(onehot, axis=0) - onehot
    position = jnp.sum(before * onehot, axis=1)
    column = flat_ids // slot_count
    slot_index = flat_ids % slot_count
    target = (slot_index * ex_count + column) * CAP + position
    placed = target[None, :] == jnp.arange(slot_rows)[:, None]
    placed_rows = placed.reshape(slot_rows, tok_rows, top_count).any(axis=2).astype(jnp.bfloat16)
    packed = jnp.dot(placed_rows, tokens, preferred_element_type=jnp.float32).astype(jnp.bfloat16)
    packed = packed.reshape(slot_count, ex_count, CAP, model_width)
    packed_gates = jnp.dot(
        placed.astype(jnp.bfloat16), gates.reshape(-1), preferred_element_type=jnp.float32
    )
    packed_gates = packed_gates.astype(jnp.bfloat16).reshape(slot_count, ex_count, CAP)
    spread = jnp.broadcast_to(
        packed[:, :, None], (slot_count, ex_count, at_count, CAP, model_width)
    )
    spread = spread.reshape(slot_count, ex_count * at_count, CAP, model_width)
    spread_gates = jnp.broadcast_to(packed_gates[:, :, None], (slot_count, ex_count, at_count, CAP))
    spread_gates = spread_gates.reshape(slot_count, ex_count * at_count, CAP)
    arrived, arrived_gates = (
        lax.all_to_all(spread, ("ex", "at"), split_axis=1, concat_axis=1, tiled=True),
        lax.all_to_all(spread_gates, ("ex", "at"), split_axis=1, concat_axis=1, tiled=True),
    )
    partial_value = expert_part(
        arrived.reshape(slot_count, -1, model_width),
        arrived_gates.reshape(slot_count, -1),
        w_in,
        w_out,
    )
    partial_value = partial_value.reshape(slot_count, ex_count * at_count, CAP, model_width)
    returned = lax.all_to_all(partial_value, ("ex", "at"), split_axis=1, concat_axis=1, tiled=True)
    out_rows = jnp.sum(
        returned.reshape(slot_count, ex_count, at_count, CAP, model_width).astype(jnp.float32),
        axis=2,
    )
    flat_out = out_rows.reshape(slot_rows, model_width)
    moe_out = jnp.sum(flat_out[target.reshape(tok_rows, top_count)], axis=1).astype(jnp.bfloat16)
    return moe_out


def per_device(
    fused, tokens, expert_ids, gates, w_in, w_out, q_latent, q_rope, cache_latent, cache_rope, lengths
):
    layer = fused_experts if fused else routed_experts
    moe_out = layer(tokens, expert_ids, gates, w_in, w_out)
    context = latent_attention(q_latent, q_rope, cache_latent, cache_rope, lengths)
    return (moe_out, context)


def solution(mesh):
    fused = mesh.shape["ex"] == 4 and mesh.shape["at"] == 4
    return jax.shard_map(
        functools.partial(per_device, fused),
        mesh=mesh,
        in_specs=(
            P(("grp", "ex", "at"), None),
            P(("grp", "ex", "at"), None),
            P(("grp", "ex", "at"), None),
            P("ex", None, None, "at"),
            P("ex", "at", None),
            P(("grp", "ex", "at"), None, None),
            P(("grp", "ex", "at"), None),
            P(("grp", "ex", "at"), None, None),
            P(("grp", "ex", "at"), None, None),
            P(("grp", "ex", "at")),
        ),
        out_specs=(P(("grp", "ex", "at"), None), P(("grp", "ex", "at"), None, None)),
        check_vma=False,
    )
```

```python
import functools

import jax
import jax.numpy as jnp
from jax import lax
from jax.experimental import pallas as pl
from jax.experimental.pallas import tpu as pltpu
from jax.sharding import PartitionSpec as P

CAP = 5
LANES = 128
D_BLOCK = 1024
W_SLOTS = 11
O_COLS = 512
O_SLOTS = 6


def moe_kernel(
    x_ref, win_ref, wout_ref, ql_ref, qr_ref, cl_ref, cp_ref, len_ref, o_ref, ctx_ref,
    xg, xe, wbuf, obuf, acc, hid, keep1, out1, in1, keep2, out2, in2, keep3, out3, in3,
    wsem, osem, zs, zr, ys, yr, cs, cr, s1, q1, s2, q2, s3, q3,
):
    experts_here, model_width, pair, hid_units = win_ref.shape
    jbs = hid_units // LANES
    win_rows = win_ref.reshape(experts_here, model_width * pair, hid_units)
    at_count = 4
    tok_rows = x_ref.shape[0]
    rows = 16 * tok_rows
    e0 = lax.axis_index("ex")
    a0 = lax.axis_index("at")
    y0 = e0 // 2
    c0 = e0 % 2
    e_y = (1 - y0) * 2 + c0
    e_c = y0 * 2 + (1 - c0)
    d_chunks = model_width // D_BLOCK
    w_chunks = experts_here * d_chunks
    o_chunks = model_width // O_COLS

    def w_copy(i, jb):
        return pltpu.make_async_copy(
            win_rows.at[
                i // d_chunks,
                pl.ds(pl.multiple_of((i % d_chunks) * 2 * D_BLOCK, 2 * D_BLOCK), 2 * D_BLOCK),
                pl.ds(jb * LANES, LANES),
            ],
            wbuf.at[i % W_SLOTS, jb],
            wsem.at[i % W_SLOTS, jb],
        )

    def o_copy(i):
        return pltpu.make_async_copy(
            wout_ref.at[:, :, pl.ds(pl.multiple_of(i * O_COLS, O_COLS), O_COLS)],
            obuf.at[i % O_SLOTS],
            osem.at[i % O_SLOTS],
        )

    def w_start(i, carry):
        for jb in range(jbs):
            w_copy(i, jb).start()
        return carry

    def o_start(i, carry):
        o_copy(i).start()
        return carry

    lax.fori_loop(0, W_SLOTS, w_start, 0)

    to_z = [{"ex": e0, "at": (a0 + j) % at_count} for j in range(at_count)]
    to_y = {"ex": e_y, "at": a0}
    to_c = {"ex": e_c, "at": a0}
    barrier = pltpu.get_barrier_semaphore()
    for peer in to_z[1:] + [to_y, to_c]:
        pl.semaphore_signal(barrier, inc=1, device_id=peer, device_id_type=pl.DeviceIdType.MESH)
    pl.semaphore_wait(barrier, at_count + 1)

    def remote(src, dst, send, recv, peer):
        return pltpu.make_async_remote_copy(
            src_ref=src, dst_ref=dst, send_sem=send, recv_sem=recv,
            device_id=peer, device_id_type=pl.DeviceIdType.MESH,
        )

    def block(ex, j):
        return ex * at_count + (a0 + at_count - j) % at_count

    def z_copy(j, slot):
        return remote(xg.at[slot], xg.at[slot], zs.at[j - 1], zr.at[j - 1], to_z[j])

    def y_copy(j, slot):
        return remote(xg.at[slot], xg.at[slot], ys.at[j], yr.at[j], to_y)

    def c_copy(j, slot):
        return remote(xg.at[slot], xg.at[slot], cs.at[j], cr.at[j], to_c)

    own = block(e0, 0)
    xg[own] = x_ref[...]
    for j in range(1, at_count):
        z_copy(j, own).start()
    y_copy(0, own).start()
    c_copy(0, own).start()
    lax.fori_loop(0, O_SLOTS, o_start, 0)
    def attend(r):
        last = (((1,), (1,)), ((), ()))
        latent = cl_ref[r]
        scores = lax.dot_general(ql_ref[r], latent, last, preferred_element_type=jnp.float32)
        scores = scores + jnp.dot(qr_ref[r], cp_ref[r], preferred_element_type=jnp.float32)
        scores = scores * 192.0 ** (-0.5)
        visible = lax.broadcasted_iota(jnp.int32, scores.shape, 1) < len_ref[r]
        scores = jnp.where(visible, scores, -1e30)
        peak = jnp.max(scores, axis=1, keepdims=True)
        expo = jnp.where(visible, jnp.exp(scores - peak), 0.0)
        probs = (expo / jnp.sum(expo, axis=1, keepdims=True)).astype(jnp.bfloat16)
        context = jnp.dot(probs, latent, preferred_element_type=jnp.float32)
        ctx_ref[r] = context.astype(jnp.bfloat16)

    att_rows = ql_ref.shape[0]
    for j in (1, 3, 2):
        if j - 1 < att_rows:
            attend(j - 1)
        z_copy(j, block(e0, j)).wait_recv()
        y_copy(j, block(e0, j)).start()
        c_copy(j, block(e0, j)).start()
    for r in range(3, att_rows):
        attend(r)
    for j in (0, 1, 3, 2):
        y_copy(j, block(e_y, j)).wait_recv()
        c_copy(4 + j, block(e_y, j)).start()
    for j in (0, 1, 3, 2):
        c_copy(j, block(e_c, j)).wait_recv()
    for j in (0, 1, 3, 2):
        c_copy(4 + j, block((1 - y0) * 2 + (1 - c0), j)).wait_recv()

    row = lax.broadcasted_iota(jnp.int32, (LANES, 2 * LANES), 0)
    col = lax.broadcasted_iota(jnp.int32, (LANES, 2 * LANES), 1)
    spread = [(col == 2 * row + p).astype(jnp.bfloat16) for p in range(2)]

    def expand(i, carry):
        x = xg[:, :, pl.ds(pl.multiple_of(i * LANES, LANES), LANES)].astype(jnp.float32)
        x = x.reshape(rows, LANES).astype(jnp.bfloat16)
        for p in range(2):
            xe[p * rows:(p + 1) * rows, pl.ds(pl.multiple_of(i * 2 * LANES, 2 * LANES), 2 * LANES)] = (
                jnp.dot(x, spread[p], preferred_element_type=jnp.float32).astype(jnp.bfloat16)
            )
        return carry

    lax.fori_loop(0, model_width // LANES, expand, 0)
    dense = xg[:, :, model_width:model_width + LANES].astype(jnp.float32).reshape(rows, LANES)
    lane = lax.broadcasted_iota(jnp.int32, (rows, LANES), 1)

    def one_expert(e, carry):
        acc[...] = jnp.zeros_like(acc)

        def step(d, inner):
            i = e * d_chunks + d
            for jb in range(jbs):
                w_copy(i, jb).wait()
            x = xe[:, pl.ds(pl.multiple_of(d * 2 * D_BLOCK, 2 * D_BLOCK), 2 * D_BLOCK)]
            w = jnp.concatenate([wbuf[i % W_SLOTS, jb] for jb in range(jbs)], axis=1)
            acc[...] += jnp.dot(x, w, preferred_element_type=jnp.float32)

            @pl.when(i + W_SLOTS < w_chunks)
            def _():
                w_start(i + W_SLOTS, 0)

            return inner

        lax.fori_loop(0, d_chunks, step, 0)
        gate = jnp.sum(jnp.where(lane == e0 * experts_here + e, dense, 0.0), axis=1, keepdims=True)
        hidden = jax.nn.silu(acc[:rows, :]) * acc[rows:, :] * gate
        hid[:, pl.ds(pl.multiple_of(e * hid_units, hid_units), hid_units)] = hidden.astype(jnp.bfloat16)
        return carry

    lax.fori_loop(0, experts_here, one_expert, 0)

    def core_copy(i):
        return remote(out1.at[i], in1.at[i], s1.at[i], q1.at[i], to_c)

    def row_copy(i):
        return remote(out2.at[i], in2.at[i], s2.at[i], q2.at[i], to_y)

    def col_copy(i, j):
        return remote(
            out3.at[i, (a0 + j) % at_count], in3.at[i, j - 1], s3.at[i, j - 1], q3.at[i, j - 1], to_z[j]
        )

    def down(i, carry):
        @pl.when(i < o_chunks)
        def _():
            o_copy(i).wait()
            w = obuf[i % O_SLOTS].reshape(experts_here * hid_units, O_COLS)
            part = jnp.dot(hid[...], w, preferred_element_type=jnp.float32)
            part = part.reshape(2, 2, rows // 4, O_COLS)
            keep1[i] = jnp.where(c0 == 0, part[:, 0], part[:, 1])
            out1[i] = jnp.where(c0 == 0, part[:, 1], part[:, 0]).astype(jnp.bfloat16)
            core_copy(i).start()

            @pl.when(i + O_SLOTS < o_chunks)
            def _():
                o_start(i + O_SLOTS, 0)

        @pl.when((i >= 1) & (i < o_chunks + 1))
        def _():
            k = i - 1
            core_copy(k).wait_recv()
            total = keep1[k] + in1[k].astype(jnp.float32)
            keep2[k] = jnp.where(y0 == 0, total[0], total[1])
            out2[k] = jnp.where(y0 == 0, total[1], total[0]).astype(jnp.bfloat16)
            row_copy(k).start()

        @pl.when((i >= 3) & (i < o_chunks + 3))
        def _():
            k = i - 3
            row_copy(k).wait_recv()
            total = keep2[k] + in2[k].astype(jnp.float32)
            total = total.reshape(at_count, tok_rows, O_COLS)
            out3[k] = total.astype(jnp.bfloat16)
            which = lax.broadcasted_iota(jnp.int32, total.shape, 0)
            keep3[k] = jnp.sum(jnp.where(which == a0, total, 0.0), axis=0)
            for j in range(1, at_count):
                col_copy(k, j).start()

        @pl.when(i >= 5)
        def _():
            k = i - 5
            for j in range(1, at_count):
                col_copy(k, j).wait_recv()
            total = keep3[k] + jnp.sum(in3[k].astype(jnp.float32), axis=0)
            o_ref[:, pl.ds(pl.multiple_of(k * O_COLS, O_COLS), O_COLS)] = total.astype(jnp.bfloat16)
            core_copy(k).wait_send()
            row_copy(k).wait_send()
            for j in range(1, at_count):
                col_copy(k, j).wait_send()

        return carry

    lax.fori_loop(0, o_chunks + 5, down, 0)
    for j in range(1, at_count):
        z_copy(j, own).wait_send()
    for j in range(at_count):
        y_copy(j, block(e0, j)).wait_send()
        c_copy(j, block(e0, j)).wait_send()
        c_copy(4 + j, block(e_y, j)).wait_send()


def fused_layers(
    tokens, expert_ids, gates, w_in, w_out, q_latent, q_rope, cache_latent, cache_rope, lengths
):
    tok_rows, model_width = tokens.shape
    slot_count, _, _, hid_units = w_in.shape
    rows = 16 * tok_rows
    chunks = model_width // O_COLS
    jbs = hid_units // LANES
    hit = expert_ids[:, :, None] == jnp.arange(LANES)[None, None, :]
    dense = jnp.sum(jnp.where(hit, gates[:, :, None], jnp.bfloat16(0)), axis=1)
    block = jnp.concatenate([tokens, dense.astype(jnp.bfloat16)], axis=1)
    rope_q = q_rope.reshape(q_latent.shape[0], q_latent.shape[1], -1)
    bf16, f32 = jnp.bfloat16, jnp.float32
    dma = pltpu.SemaphoreType.DMA
    return pl.pallas_call(
        moe_kernel,
        out_shape=(
            jax.ShapeDtypeStruct((tok_rows, model_width), bf16),
            jax.ShapeDtypeStruct(q_latent.shape, bf16),
        ),
        in_specs=[
            pl.BlockSpec(memory_space=pltpu.VMEM),
            pl.BlockSpec(memory_space=pl.ANY),
            pl.BlockSpec(memory_space=pl.ANY),
            pl.BlockSpec(memory_space=pltpu.VMEM),
            pl.BlockSpec(memory_space=pltpu.VMEM),
            pl.BlockSpec(memory_space=pltpu.VMEM),
            pl.BlockSpec(memory_space=pltpu.VMEM),
            pl.BlockSpec(memory_space=pltpu.SMEM),
        ],
        out_specs=(
            pl.BlockSpec(memory_space=pltpu.VMEM),
            pl.BlockSpec(memory_space=pltpu.VMEM),
        ),
        scratch_shapes=[
            pltpu.VMEM((16, tok_rows, model_width + LANES), bf16),
            pltpu.VMEM((2 * rows, 2 * model_width), bf16),
            pltpu.VMEM((W_SLOTS, jbs, 2 * D_BLOCK, LANES), bf16),
            pltpu.VMEM((O_SLOTS, slot_count, hid_units, O_COLS), bf16),
            pltpu.VMEM((2 * rows, hid_units), f32),
            pltpu.VMEM((rows, slot_count * hid_units), bf16),
            pltpu.VMEM((chunks, 2, rows // 4, O_COLS), f32),
            pltpu.VMEM((chunks, 2, rows // 4, O_COLS), bf16),
            pltpu.VMEM((chunks, 2, rows // 4, O_COLS), bf16),
            pltpu.VMEM((chunks, rows // 4, O_COLS), f32),
            pltpu.VMEM((chunks, rows // 4, O_COLS), bf16),
            pltpu.VMEM((chunks, rows // 4, O_COLS), bf16),
            pltpu.VMEM((chunks, tok_rows, O_COLS), f32),
            pltpu.VMEM((chunks, 4, tok_rows, O_COLS), bf16),
            pltpu.VMEM((chunks, 3, tok_rows, O_COLS), bf16),
            dma((W_SLOTS, jbs)), dma((O_SLOTS,)),
            dma((3,)), dma((3,)), dma((4,)), dma((4,)), dma((8,)), dma((8,)),
            dma((chunks,)), dma((chunks,)), dma((chunks,)), dma((chunks,)),
            dma((chunks, 3)), dma((chunks, 3)),
        ],
        compiler_params=pltpu.CompilerParams(
            collective_id=0, has_side_effects=True, vmem_limit_bytes=61 << 20
        ),
    )(block, w_in, w_out, q_latent, rope_q, cache_latent, cache_rope, lengths)


def expert_part(row_block, row_gates, w_in, w_out):
    slot_count, model_width, pair_count, hid_units = w_in.shape
    gate_up = jnp.einsum(
        "srd,sdf->srf",
        row_block,
        w_in.reshape(slot_count, model_width, pair_count * hid_units),
        preferred_element_type=jnp.float32,
    )
    hidden = (jax.nn.silu(gate_up[..., :hid_units]) * gate_up[..., hid_units:]).astype(jnp.bfloat16)
    down_out = jnp.einsum("srf,sfd->srd", hidden, w_out, preferred_element_type=jnp.float32)
    return (down_out * row_gates[..., None].astype(jnp.float32)).astype(jnp.bfloat16)


def latent_attention(q_latent, q_rope, cache_latent, cache_rope, lengths):
    att_rows, head_count, latent_width = q_latent.shape
    positions = cache_latent.shape[1]
    rope_q = q_rope.reshape(att_rows, head_count, -1)
    scores = jnp.einsum("ahl,acl->ahc", q_latent, cache_latent, preferred_element_type=jnp.float32)
    scores = scores + jnp.einsum(
        "ahr,arc->ahc", rope_q, cache_rope, preferred_element_type=jnp.float32
    )
    scores = scores * 192.0 ** (-0.5)
    visible = jnp.arange(positions)[None, None, :] < lengths[:, None, None]
    scores = jnp.where(visible, scores, -1e30)
    peak = jnp.max(scores, axis=2, keepdims=True)
    expo = jnp.where(visible, jnp.exp(scores - peak), 0.0)
    probs = (expo / jnp.sum(expo, axis=2, keepdims=True)).astype(jnp.bfloat16)
    context = jnp.einsum("ahc,acl->ahl", probs, cache_latent, preferred_element_type=jnp.float32)
    return context.astype(jnp.bfloat16)


def routed_experts(
    tokens, expert_ids, gates, w_in, w_out
):
    tok_rows, model_width = tokens.shape
    top_count = expert_ids.shape[1]
    slot_count = w_in.shape[0]
    ex_count = lax.axis_size("ex")
    at_count = lax.axis_size("at")
    experts = slot_count * ex_count
    slot_rows = experts * CAP
    flat_ids = expert_ids.reshape(-1)
    onehot = (flat_ids[:, None] == jnp.arange(experts)[None, :]).astype(jnp.int32)
    before = jnp.cumsum(onehot, axis=0) - onehot
    position = jnp.sum(before * onehot, axis=1)
    column = flat_ids // slot_count
    slot_index = flat_ids % slot_count
    target = (slot_index * ex_count + column) * CAP + position
    placed = target[None, :] == jnp.arange(slot_rows)[:, None]
    placed_rows = placed.reshape(slot_rows, tok_rows, top_count).any(axis=2).astype(jnp.bfloat16)
    packed = jnp.dot(placed_rows, tokens, preferred_element_type=jnp.float32).astype(jnp.bfloat16)
    packed = packed.reshape(slot_count, ex_count, CAP, model_width)
    packed_gates = jnp.dot(
        placed.astype(jnp.bfloat16), gates.reshape(-1), preferred_element_type=jnp.float32
    )
    packed_gates = packed_gates.astype(jnp.bfloat16).reshape(slot_count, ex_count, CAP)
    spread = jnp.broadcast_to(
        packed[:, :, None], (slot_count, ex_count, at_count, CAP, model_width)
    )
    spread = spread.reshape(slot_count, ex_count * at_count, CAP, model_width)
    spread_gates = jnp.broadcast_to(packed_gates[:, :, None], (slot_count, ex_count, at_count, CAP))
    spread_gates = spread_gates.reshape(slot_count, ex_count * at_count, CAP)
    arrived, arrived_gates = (
        lax.all_to_all(spread, ("ex", "at"), split_axis=1, concat_axis=1, tiled=True),
        lax.all_to_all(spread_gates, ("ex", "at"), split_axis=1, concat_axis=1, tiled=True),
    )
    partial_value = expert_part(
        arrived.reshape(slot_count, -1, model_width),
        arrived_gates.reshape(slot_count, -1),
        w_in,
        w_out,
    )
    partial_value = partial_value.reshape(slot_count, ex_count * at_count, CAP, model_width)
    returned = lax.all_to_all(partial_value, ("ex", "at"), split_axis=1, concat_axis=1, tiled=True)
    out_rows = jnp.sum(
        returned.reshape(slot_count, ex_count, at_count, CAP, model_width).astype(jnp.float32),
        axis=2,
    )
    flat_out = out_rows.reshape(slot_rows, model_width)
    moe_out = jnp.sum(flat_out[target.reshape(tok_rows, top_count)], axis=1).astype(jnp.bfloat16)
    return moe_out


def per_device(
    fused, tokens, expert_ids, gates, w_in, w_out, q_latent, q_rope, cache_latent, cache_rope, lengths
):
    if fused:
        return fused_layers(
            tokens, expert_ids, gates, w_in, w_out, q_latent, q_rope, cache_latent, cache_rope, lengths
        )
    moe_out = routed_experts(tokens, expert_ids, gates, w_in, w_out)
    context = latent_attention(q_latent, q_rope, cache_latent, cache_rope, lengths)
    return (moe_out, context)


def solution(mesh):
    fused = mesh.shape["ex"] == 4 and mesh.shape["at"] == 4
    return jax.shard_map(
        functools.partial(per_device, fused),
        mesh=mesh,
        in_specs=(
            P(("grp", "ex", "at"), None),
            P(("grp", "ex", "at"), None),
            P(("grp", "ex", "at"), None),
            P("ex", None, None, "at"),
            P("ex", "at", None),
            P(("grp", "ex", "at"), None, None),
            P(("grp", "ex", "at"), None),
            P(("grp", "ex", "at"), None, None),
            P(("grp", "ex", "at"), None, None),
            P(("grp", "ex", "at")),
        ),
        out_specs=(P(("grp", "ex", "at"), None), P(("grp", "ex", "at"), None, None)),
        check_vma=False,
    )
```

```python
import functools

import jax
import jax.numpy as jnp
from jax import lax
from jax.experimental import pallas as pl
from jax.experimental.pallas import tpu as pltpu
from jax.sharding import PartitionSpec as P

CAP = 5
LANES = 128
D_BLOCK = 1024
W_SLOTS = 11
O_COLS = 512
O_SLOTS = 6


def moe_kernel(
    x_ref, win_ref, wout_ref, ql_ref, qr_ref, cl_ref, cp_ref, len_ref, o_ref, ctx_ref,
    xg, xe, wbuf, obuf, acc, hid, keep1, out1, in1, keep2, out2, in2, keep3, out3, in3,
    wsem, osem, zs, zr, ys, yr, cs, cr, s1, q1, s2, q2, s3, q3,
):
    experts_here, model_width, pair, hid_units = win_ref.shape
    jbs = hid_units // LANES
    win_rows = win_ref.reshape(experts_here, model_width * pair, hid_units)
    at_count = 4
    tok_rows = x_ref.shape[0]
    rows = 16 * tok_rows
    e0 = lax.axis_index("ex")
    a0 = lax.axis_index("at")
    y0 = e0 // 2
    c0 = e0 % 2
    e_y = (1 - y0) * 2 + c0
    e_c = y0 * 2 + (1 - c0)
    d_chunks = model_width // D_BLOCK
    w_chunks = experts_here * d_chunks
    o_chunks = model_width // O_COLS

    def w_copy(i, jb):
        return pltpu.make_async_copy(
            win_rows.at[
                i // d_chunks,
                pl.ds(pl.multiple_of((i % d_chunks) * 2 * D_BLOCK, 2 * D_BLOCK), 2 * D_BLOCK),
                pl.ds(jb * LANES, LANES),
            ],
            wbuf.at[i % W_SLOTS, jb],
            wsem.at[i % W_SLOTS, jb],
        )

    def o_copy(i):
        return pltpu.make_async_copy(
            wout_ref.at[:, :, pl.ds(pl.multiple_of(i * O_COLS, O_COLS), O_COLS)],
            obuf.at[i % O_SLOTS],
            osem.at[i % O_SLOTS],
        )

    def w_start(i, carry):
        for jb in range(jbs):
            w_copy(i, jb).start()
        return carry

    def o_start(i, carry):
        o_copy(i).start()
        return carry

    lax.fori_loop(0, W_SLOTS, w_start, 0)

    to_z = [{"ex": e0, "at": (a0 + j) % at_count} for j in range(at_count)]
    to_y = {"ex": e_y, "at": a0}
    to_c = {"ex": e_c, "at": a0}
    barrier = pltpu.get_barrier_semaphore()
    for peer in to_z[1:] + [to_y, to_c]:
        pl.semaphore_signal(barrier, inc=1, device_id=peer, device_id_type=pl.DeviceIdType.MESH)
    pl.semaphore_wait(barrier, at_count + 1)

    def remote(src, dst, send, recv, peer):
        return pltpu.make_async_remote_copy(
            src_ref=src, dst_ref=dst, send_sem=send, recv_sem=recv,
            device_id=peer, device_id_type=pl.DeviceIdType.MESH,
        )

    def block(ex, j):
        return ex * at_count + (a0 + at_count - j) % at_count

    def z_copy(j, slot):
        return remote(xg.at[slot], xg.at[slot], zs.at[j - 1], zr.at[j - 1], to_z[j])

    def y_copy(j, slot):
        return remote(xg.at[slot], xg.at[slot], ys.at[j], yr.at[j], to_y)

    def c_copy(j, slot):
        return remote(xg.at[slot], xg.at[slot], cs.at[j], cr.at[j], to_c)

    own = block(e0, 0)
    xg[own] = x_ref[...]
    for j in range(1, at_count):
        z_copy(j, own).start()
    y_copy(0, own).start()
    c_copy(0, own).start()
    lax.fori_loop(0, O_SLOTS, o_start, 0)
    def attend(r):
        last = (((1,), (1,)), ((), ()))
        latent = cl_ref[r]
        scores = lax.dot_general(ql_ref[r], latent, last, preferred_element_type=jnp.float32)
        scores = scores + jnp.dot(qr_ref[r], cp_ref[r], preferred_element_type=jnp.float32)
        scores = scores * 192.0 ** (-0.5)
        visible = lax.broadcasted_iota(jnp.int32, scores.shape, 1) < len_ref[r]
        scores = jnp.where(visible, scores, -1e30)
        peak = jnp.max(scores, axis=1, keepdims=True)
        expo = jnp.where(visible, jnp.exp(scores - peak), 0.0)
        probs = (expo / jnp.sum(expo, axis=1, keepdims=True)).astype(jnp.bfloat16)
        context = jnp.dot(probs, latent, preferred_element_type=jnp.float32)
        ctx_ref[r] = context.astype(jnp.bfloat16)

    att_rows = ql_ref.shape[0]
    for j in (1, 3, 2):
        if j - 1 < att_rows:
            attend(j - 1)
        z_copy(j, block(e0, j)).wait_recv()
        y_copy(j, block(e0, j)).start()
        c_copy(j, block(e0, j)).start()
    for r in range(3, att_rows):
        attend(r)
    for j in (0, 1, 3, 2):
        y_copy(j, block(e_y, j)).wait_recv()
        c_copy(4 + j, block(e_y, j)).start()
    for j in (0, 1, 3, 2):
        c_copy(j, block(e_c, j)).wait_recv()
    for j in (0, 1, 3, 2):
        c_copy(4 + j, block((1 - y0) * 2 + (1 - c0), j)).wait_recv()

    row = lax.broadcasted_iota(jnp.int32, (LANES, 2 * LANES), 0)
    col = lax.broadcasted_iota(jnp.int32, (LANES, 2 * LANES), 1)
    spread = [(col == 2 * row + p).astype(jnp.bfloat16) for p in range(2)]

    group = 8

    def expand(g, carry):
        for u in range(group):
            i = g * group + u
            x = xg[:, :, pl.ds(pl.multiple_of(i * LANES, LANES), LANES)].astype(jnp.float32)
            x = x.reshape(rows, LANES).astype(jnp.bfloat16)
            wide = pl.ds(pl.multiple_of(i * 2 * LANES, 2 * LANES), 2 * LANES)
            for p in range(2):
                xe[p * rows:(p + 1) * rows, wide] = jnp.dot(
                    x, spread[p], preferred_element_type=jnp.float32
                ).astype(jnp.bfloat16)
        return carry

    lax.fori_loop(0, model_width // (LANES * group), expand, 0)
    dense = xg[:, :, model_width:model_width + LANES].astype(jnp.float32).reshape(rows, LANES)
    lane = lax.broadcasted_iota(jnp.int32, (rows, LANES), 1)

    def one_expert(e, carry):
        acc[...] = jnp.zeros_like(acc)

        def step(d, inner):
            i = e * d_chunks + d
            for jb in range(jbs):
                w_copy(i, jb).wait()
            x = xe[:, pl.ds(pl.multiple_of(d * 2 * D_BLOCK, 2 * D_BLOCK), 2 * D_BLOCK)]
            w = jnp.concatenate([wbuf[i % W_SLOTS, jb] for jb in range(jbs)], axis=1)
            acc[...] += jnp.dot(x, w, preferred_element_type=jnp.float32)

            @pl.when(i + W_SLOTS < w_chunks)
            def _():
                w_start(i + W_SLOTS, 0)

            return inner

        lax.fori_loop(0, d_chunks, step, 0)
        gate = jnp.sum(jnp.where(lane == e0 * experts_here + e, dense, 0.0), axis=1, keepdims=True)
        hidden = jax.nn.silu(acc[:rows, :]) * acc[rows:, :] * gate
        hid[:, pl.ds(pl.multiple_of(e * hid_units, hid_units), hid_units)] = hidden.astype(jnp.bfloat16)
        return carry

    lax.fori_loop(0, experts_here, one_expert, 0)

    def core_copy(i):
        return remote(out1.at[i], in1.at[i], s1.at[i], q1.at[i], to_c)

    def row_copy(i):
        return remote(out2.at[i], in2.at[i], s2.at[i], q2.at[i], to_y)

    def col_copy(i, j):
        return remote(
            out3.at[i, (a0 + j) % at_count], in3.at[i, j - 1], s3.at[i, j - 1], q3.at[i, j - 1], to_z[j]
        )

    def down(i, carry):
        @pl.when(i < o_chunks)
        def _():
            o_copy(i).wait()
            w = obuf[i % O_SLOTS].reshape(experts_here * hid_units, O_COLS)
            part = jnp.dot(hid[...], w, preferred_element_type=jnp.float32)
            part = part.reshape(2, 2, rows // 4, O_COLS)
            keep1[i] = jnp.where(c0 == 0, part[:, 0], part[:, 1])
            out1[i] = jnp.where(c0 == 0, part[:, 1], part[:, 0]).astype(jnp.bfloat16)
            core_copy(i).start()

            @pl.when(i + O_SLOTS < o_chunks)
            def _():
                o_start(i + O_SLOTS, 0)

        @pl.when((i >= 1) & (i < o_chunks + 1))
        def _():
            k = i - 1
            core_copy(k).wait_recv()
            total = keep1[k] + in1[k].astype(jnp.float32)
            keep2[k] = jnp.where(y0 == 0, total[0], total[1])
            out2[k] = jnp.where(y0 == 0, total[1], total[0]).astype(jnp.bfloat16)
            row_copy(k).start()

        @pl.when((i >= 3) & (i < o_chunks + 3))
        def _():
            k = i - 3
            row_copy(k).wait_recv()
            total = keep2[k] + in2[k].astype(jnp.float32)
            total = total.reshape(at_count, tok_rows, O_COLS)
            out3[k] = total.astype(jnp.bfloat16)
            which = lax.broadcasted_iota(jnp.int32, total.shape, 0)
            keep3[k] = jnp.sum(jnp.where(which == a0, total, 0.0), axis=0)
            for j in range(1, at_count):
                col_copy(k, j).start()

        @pl.when(i >= 5)
        def _():
            k = i - 5
            for j in range(1, at_count):
                col_copy(k, j).wait_recv()
            total = keep3[k] + jnp.sum(in3[k].astype(jnp.float32), axis=0)
            o_ref[:, pl.ds(pl.multiple_of(k * O_COLS, O_COLS), O_COLS)] = total.astype(jnp.bfloat16)
            core_copy(k).wait_send()
            row_copy(k).wait_send()
            for j in range(1, at_count):
                col_copy(k, j).wait_send()

        return carry

    lax.fori_loop(0, o_chunks + 5, down, 0)
    for j in range(1, at_count):
        z_copy(j, own).wait_send()
    for j in range(at_count):
        y_copy(j, block(e0, j)).wait_send()
        c_copy(j, block(e0, j)).wait_send()
        c_copy(4 + j, block(e_y, j)).wait_send()


def fused_layers(
    tokens, expert_ids, gates, w_in, w_out, q_latent, q_rope, cache_latent, cache_rope, lengths
):
    tok_rows, model_width = tokens.shape
    slot_count, _, _, hid_units = w_in.shape
    rows = 16 * tok_rows
    chunks = model_width // O_COLS
    jbs = hid_units // LANES
    hit = expert_ids[:, :, None] == jnp.arange(LANES)[None, None, :]
    dense = jnp.sum(jnp.where(hit, gates[:, :, None], jnp.bfloat16(0)), axis=1)
    block = jnp.concatenate([tokens, dense.astype(jnp.bfloat16)], axis=1)
    rope_q = q_rope.reshape(q_latent.shape[0], q_latent.shape[1], -1)
    bf16, f32 = jnp.bfloat16, jnp.float32
    dma = pltpu.SemaphoreType.DMA
    return pl.pallas_call(
        moe_kernel,
        out_shape=(
            jax.ShapeDtypeStruct((tok_rows, model_width), bf16),
            jax.ShapeDtypeStruct(q_latent.shape, bf16),
        ),
        in_specs=[
            pl.BlockSpec(memory_space=pltpu.VMEM),
            pl.BlockSpec(memory_space=pl.ANY),
            pl.BlockSpec(memory_space=pl.ANY),
            pl.BlockSpec(memory_space=pltpu.VMEM),
            pl.BlockSpec(memory_space=pltpu.VMEM),
            pl.BlockSpec(memory_space=pltpu.VMEM),
            pl.BlockSpec(memory_space=pltpu.VMEM),
            pl.BlockSpec(memory_space=pltpu.SMEM),
        ],
        out_specs=(
            pl.BlockSpec(memory_space=pltpu.VMEM),
            pl.BlockSpec(memory_space=pltpu.VMEM),
        ),
        scratch_shapes=[
            pltpu.VMEM((16, tok_rows, model_width + LANES), bf16),
            pltpu.VMEM((2 * rows, 2 * model_width), bf16),
            pltpu.VMEM((W_SLOTS, jbs, 2 * D_BLOCK, LANES), bf16),
            pltpu.VMEM((O_SLOTS, slot_count, hid_units, O_COLS), bf16),
            pltpu.VMEM((2 * rows, hid_units), f32),
            pltpu.VMEM((rows, slot_count * hid_units), bf16),
            pltpu.VMEM((chunks, 2, rows // 4, O_COLS), f32),
            pltpu.VMEM((chunks, 2, rows // 4, O_COLS), bf16),
            pltpu.VMEM((chunks, 2, rows // 4, O_COLS), bf16),
            pltpu.VMEM((chunks, rows // 4, O_COLS), f32),
            pltpu.VMEM((chunks, rows // 4, O_COLS), bf16),
            pltpu.VMEM((chunks, rows // 4, O_COLS), bf16),
            pltpu.VMEM((chunks, tok_rows, O_COLS), f32),
            pltpu.VMEM((chunks, 4, tok_rows, O_COLS), bf16),
            pltpu.VMEM((chunks, 3, tok_rows, O_COLS), bf16),
            dma((W_SLOTS, jbs)), dma((O_SLOTS,)),
            dma((3,)), dma((3,)), dma((4,)), dma((4,)), dma((8,)), dma((8,)),
            dma((chunks,)), dma((chunks,)), dma((chunks,)), dma((chunks,)),
            dma((chunks, 3)), dma((chunks, 3)),
        ],
        compiler_params=pltpu.CompilerParams(
            collective_id=0, has_side_effects=True, vmem_limit_bytes=61 << 20
        ),
    )(block, w_in, w_out, q_latent, rope_q, cache_latent, cache_rope, lengths)


def expert_part(row_block, row_gates, w_in, w_out):
    slot_count, model_width, pair_count, hid_units = w_in.shape
    gate_up = jnp.einsum(
        "srd,sdf->srf",
        row_block,
        w_in.reshape(slot_count, model_width, pair_count * hid_units),
        preferred_element_type=jnp.float32,
    )
    hidden = (jax.nn.silu(gate_up[..., :hid_units]) * gate_up[..., hid_units:]).astype(jnp.bfloat16)
    down_out = jnp.einsum("srf,sfd->srd", hidden, w_out, preferred_element_type=jnp.float32)
    return (down_out * row_gates[..., None].astype(jnp.float32)).astype(jnp.bfloat16)


def latent_attention(q_latent, q_rope, cache_latent, cache_rope, lengths):
    att_rows, head_count, latent_width = q_latent.shape
    positions = cache_latent.shape[1]
    rope_q = q_rope.reshape(att_rows, head_count, -1)
    scores = jnp.einsum("ahl,acl->ahc", q_latent, cache_latent, preferred_element_type=jnp.float32)
    scores = scores + jnp.einsum(
        "ahr,arc->ahc", rope_q, cache_rope, preferred_element_type=jnp.float32
    )
    scores = scores * 192.0 ** (-0.5)
    visible = jnp.arange(positions)[None, None, :] < lengths[:, None, None]
    scores = jnp.where(visible, scores, -1e30)
    peak = jnp.max(scores, axis=2, keepdims=True)
    expo = jnp.where(visible, jnp.exp(scores - peak), 0.0)
    probs = (expo / jnp.sum(expo, axis=2, keepdims=True)).astype(jnp.bfloat16)
    context = jnp.einsum("ahc,acl->ahl", probs, cache_latent, preferred_element_type=jnp.float32)
    return context.astype(jnp.bfloat16)


def routed_experts(
    tokens, expert_ids, gates, w_in, w_out
):
    tok_rows, model_width = tokens.shape
    top_count = expert_ids.shape[1]
    slot_count = w_in.shape[0]
    ex_count = lax.axis_size("ex")
    at_count = lax.axis_size("at")
    experts = slot_count * ex_count
    slot_rows = experts * CAP
    flat_ids = expert_ids.reshape(-1)
    onehot = (flat_ids[:, None] == jnp.arange(experts)[None, :]).astype(jnp.int32)
    before = jnp.cumsum(onehot, axis=0) - onehot
    position = jnp.sum(before * onehot, axis=1)
    column = flat_ids // slot_count
    slot_index = flat_ids % slot_count
    target = (slot_index * ex_count + column) * CAP + position
    placed = target[None, :] == jnp.arange(slot_rows)[:, None]
    placed_rows = placed.reshape(slot_rows, tok_rows, top_count).any(axis=2).astype(jnp.bfloat16)
    packed = jnp.dot(placed_rows, tokens, preferred_element_type=jnp.float32).astype(jnp.bfloat16)
    packed = packed.reshape(slot_count, ex_count, CAP, model_width)
    packed_gates = jnp.dot(
        placed.astype(jnp.bfloat16), gates.reshape(-1), preferred_element_type=jnp.float32
    )
    packed_gates = packed_gates.astype(jnp.bfloat16).reshape(slot_count, ex_count, CAP)
    spread = jnp.broadcast_to(
        packed[:, :, None], (slot_count, ex_count, at_count, CAP, model_width)
    )
    spread = spread.reshape(slot_count, ex_count * at_count, CAP, model_width)
    spread_gates = jnp.broadcast_to(packed_gates[:, :, None], (slot_count, ex_count, at_count, CAP))
    spread_gates = spread_gates.reshape(slot_count, ex_count * at_count, CAP)
    arrived, arrived_gates = (
        lax.all_to_all(spread, ("ex", "at"), split_axis=1, concat_axis=1, tiled=True),
        lax.all_to_all(spread_gates, ("ex", "at"), split_axis=1, concat_axis=1, tiled=True),
    )
    partial_value = expert_part(
        arrived.reshape(slot_count, -1, model_width),
        arrived_gates.reshape(slot_count, -1),
        w_in,
        w_out,
    )
    partial_value = partial_value.reshape(slot_count, ex_count * at_count, CAP, model_width)
    returned = lax.all_to_all(partial_value, ("ex", "at"), split_axis=1, concat_axis=1, tiled=True)
    out_rows = jnp.sum(
        returned.reshape(slot_count, ex_count, at_count, CAP, model_width).astype(jnp.float32),
        axis=2,
    )
    flat_out = out_rows.reshape(slot_rows, model_width)
    moe_out = jnp.sum(flat_out[target.reshape(tok_rows, top_count)], axis=1).astype(jnp.bfloat16)
    return moe_out


def per_device(
    fused, tokens, expert_ids, gates, w_in, w_out, q_latent, q_rope, cache_latent, cache_rope, lengths
):
    if fused:
        return fused_layers(
            tokens, expert_ids, gates, w_in, w_out, q_latent, q_rope, cache_latent, cache_rope, lengths
        )
    moe_out = routed_experts(tokens, expert_ids, gates, w_in, w_out)
    context = latent_attention(q_latent, q_rope, cache_latent, cache_rope, lengths)
    return (moe_out, context)


def solution(mesh):
    fused = mesh.shape["ex"] == 4 and mesh.shape["at"] == 4
    return jax.shard_map(
        functools.partial(per_device, fused),
        mesh=mesh,
        in_specs=(
            P(("grp", "ex", "at"), None),
            P(("grp", "ex", "at"), None),
            P(("grp", "ex", "at"), None),
            P("ex", None, None, "at"),
            P("ex", "at", None),
            P(("grp", "ex", "at"), None, None),
            P(("grp", "ex", "at"), None),
            P(("grp", "ex", "at"), None, None),
            P(("grp", "ex", "at"), None, None),
            P(("grp", "ex", "at")),
        ),
        out_specs=(P(("grp", "ex", "at"), None), P(("grp", "ex", "at"), None, None)),
        check_vma=False,
    )
```

```python
import functools

import jax
import jax.numpy as jnp
from jax import lax
from jax.experimental import pallas as pl
from jax.experimental.pallas import tpu as pltpu
from jax.sharding import PartitionSpec as P

CAP = 5
LANES = 128
D_BLOCK = 1024
W_SLOTS = 11
O_COLS = 512
O_SLOTS = 6


def moe_kernel(
    x_ref, win_ref, wout_ref, ql_ref, qr_ref, cl_ref, cp_ref, len_ref, o_ref, ctx_ref,
    xg, xe, wbuf, obuf, acc, hid, keep1, out1, in1, keep2, out2, in2, keep3, out3, in3,
    wsem, osem, zs, zr, ys, yr, cs, cr, s1, q1, s2, q2, s3, q3,
):
    experts_here, model_width, pair, hid_units = win_ref.shape
    jbs = hid_units // LANES
    win_rows = win_ref.reshape(experts_here, model_width * pair, hid_units)
    at_count = 4
    tok_rows = x_ref.shape[0]
    rows = 16 * tok_rows
    e0 = lax.axis_index("ex")
    a0 = lax.axis_index("at")
    y0 = e0 // 2
    c0 = e0 % 2
    e_y = (1 - y0) * 2 + c0
    e_c = y0 * 2 + (1 - c0)
    d_chunks = model_width // D_BLOCK
    w_chunks = experts_here * d_chunks
    o_chunks = model_width // O_COLS

    def w_copy(i, jb):
        return pltpu.make_async_copy(
            win_rows.at[
                i // d_chunks,
                pl.ds(pl.multiple_of((i % d_chunks) * 2 * D_BLOCK, 2 * D_BLOCK), 2 * D_BLOCK),
                pl.ds(jb * LANES, LANES),
            ],
            wbuf.at[i % W_SLOTS, jb],
            wsem.at[i % W_SLOTS, jb],
        )

    def o_copy(i):
        return pltpu.make_async_copy(
            wout_ref.at[:, :, pl.ds(pl.multiple_of(i * O_COLS, O_COLS), O_COLS)],
            obuf.at[i % O_SLOTS],
            osem.at[i % O_SLOTS],
        )

    def w_start(i, carry):
        for jb in range(jbs):
            w_copy(i, jb).start()
        return carry

    def o_start(i, carry):
        o_copy(i).start()
        return carry

    lax.fori_loop(0, W_SLOTS, w_start, 0)

    to_z = [{"ex": e0, "at": (a0 + j) % at_count} for j in range(at_count)]
    to_y = {"ex": e_y, "at": a0}
    to_c = {"ex": e_c, "at": a0}
    barrier = pltpu.get_barrier_semaphore()
    for peer in to_z[1:] + [to_y, to_c]:
        pl.semaphore_signal(barrier, inc=1, device_id=peer, device_id_type=pl.DeviceIdType.MESH)
    pl.semaphore_wait(barrier, at_count + 1)

    def remote(src, dst, send, recv, peer):
        return pltpu.make_async_remote_copy(
            src_ref=src, dst_ref=dst, send_sem=send, recv_sem=recv,
            device_id=peer, device_id_type=pl.DeviceIdType.MESH,
        )

    def block(ex, j):
        return ex * at_count + (a0 + at_count - j) % at_count

    def z_copy(j, slot):
        return remote(xg.at[slot], xg.at[slot], zs.at[j - 1], zr.at[j - 1], to_z[j])

    def y_copy(j, slot):
        return remote(xg.at[slot], xg.at[slot], ys.at[j], yr.at[j], to_y)

    def c_copy(j, slot):
        return remote(xg.at[slot], xg.at[slot], cs.at[j], cr.at[j], to_c)

    own = block(e0, 0)
    xg[own] = x_ref[...]
    for j in range(1, at_count):
        z_copy(j, own).start()
    y_copy(0, own).start()
    c_copy(0, own).start()
    lax.fori_loop(0, O_SLOTS, o_start, 0)
    def attend(r):
        last = (((1,), (1,)), ((), ()))
        latent = cl_ref[r]
        scores = lax.dot_general(ql_ref[r], latent, last, preferred_element_type=jnp.float32)
        scores = scores + jnp.dot(qr_ref[r], cp_ref[r], preferred_element_type=jnp.float32)
        scores = scores * 192.0 ** (-0.5)
        visible = lax.broadcasted_iota(jnp.int32, scores.shape, 1) < len_ref[r]
        scores = jnp.where(visible, scores, -1e30)
        peak = jnp.max(scores, axis=1, keepdims=True)
        expo = jnp.where(visible, jnp.exp(scores - peak), 0.0)
        probs = (expo / jnp.sum(expo, axis=1, keepdims=True)).astype(jnp.bfloat16)
        context = jnp.dot(probs, latent, preferred_element_type=jnp.float32)
        ctx_ref[r] = context.astype(jnp.bfloat16)

    att_rows = ql_ref.shape[0]
    for j in (1, 3, 2):
        if j - 1 < att_rows:
            attend(j - 1)
        z_copy(j, block(e0, j)).wait_recv()
        y_copy(j, block(e0, j)).start()
        c_copy(j, block(e0, j)).start()
    for r in range(3, att_rows):
        attend(r)
    for j in (0, 1, 3, 2):
        y_copy(j, block(e_y, j)).wait_recv()
        c_copy(4 + j, block(e_y, j)).start()
    for j in (0, 1, 3, 2):
        c_copy(j, block(e_c, j)).wait_recv()
    for j in (0, 1, 3, 2):
        c_copy(4 + j, block((1 - y0) * 2 + (1 - c0), j)).wait_recv()

    row = lax.broadcasted_iota(jnp.int32, (LANES, 2 * LANES), 0)
    col = lax.broadcasted_iota(jnp.int32, (LANES, 2 * LANES), 1)
    spread = [(col == 2 * row + p).astype(jnp.bfloat16) for p in range(2)]

    group = 8

    def expand(g, carry):
        for u in range(group):
            i = g * group + u
            x = xg[:, :, pl.ds(pl.multiple_of(i * LANES, LANES), LANES)].astype(jnp.float32)
            x = x.reshape(rows, LANES).astype(jnp.bfloat16)
            wide = pl.ds(pl.multiple_of(i * 2 * LANES, 2 * LANES), 2 * LANES)
            for p in range(2):
                xe[p * rows:(p + 1) * rows, wide] = jnp.dot(
                    x, spread[p], preferred_element_type=jnp.float32
                ).astype(jnp.bfloat16)
        return carry

    lax.fori_loop(0, model_width // (LANES * group), expand, 0)
    dense = xg[:, :, model_width:model_width + LANES].astype(jnp.float32).reshape(rows, LANES)
    lane = lax.broadcasted_iota(jnp.int32, (rows, LANES), 1)

    def one_expert(e, carry):
        acc[...] = jnp.zeros_like(acc)

        def step(d, inner):
            i = e * d_chunks + d
            for jb in range(jbs):
                w_copy(i, jb).wait()
            x = xe[:, pl.ds(pl.multiple_of(d * 2 * D_BLOCK, 2 * D_BLOCK), 2 * D_BLOCK)]
            w = jnp.concatenate([wbuf[i % W_SLOTS, jb] for jb in range(jbs)], axis=1)
            acc[...] += jnp.dot(x, w, preferred_element_type=jnp.float32)

            @pl.when(i + W_SLOTS < w_chunks)
            def _():
                w_start(i + W_SLOTS, 0)

            return inner

        lax.fori_loop(0, d_chunks, step, 0)
        gate = jnp.sum(jnp.where(lane == e0 * experts_here + e, dense, 0.0), axis=1, keepdims=True)
        hidden = jax.nn.silu(acc[:rows, :]) * acc[rows:, :] * gate
        hid[:, pl.ds(pl.multiple_of(e * hid_units, hid_units), hid_units)] = hidden.astype(jnp.bfloat16)
        return carry

    lax.fori_loop(0, experts_here, one_expert, 0)

    def core_copy(i):
        return remote(out1.at[i], in1.at[i], s1.at[i], q1.at[i], to_c)

    def row_copy(i):
        return remote(out2.at[i], in2.at[i], s2.at[i], q2.at[i], to_y)

    def col_copy(i, j):
        return remote(
            out3.at[i, (a0 + j) % at_count], in3.at[i, j - 1], s3.at[i, j - 1], q3.at[i, j - 1], to_z[j]
        )

    def down(i, carry):
        @pl.when(i < o_chunks)
        def _():
            o_copy(i).wait()
            w = obuf[i % O_SLOTS].reshape(experts_here * hid_units, O_COLS)
            part = jnp.dot(hid[...], w, preferred_element_type=jnp.float32)
            part = part.reshape(2, 2, rows // 4, O_COLS)
            keep1[i] = jnp.where(c0 == 0, part[:, 0], part[:, 1])
            out1[i] = jnp.where(c0 == 0, part[:, 1], part[:, 0]).astype(jnp.bfloat16)
            core_copy(i).start()

            @pl.when(i + O_SLOTS < o_chunks)
            def _():
                o_start(i + O_SLOTS, 0)

        @pl.when((i >= 2) & (i < o_chunks + 2))
        def _():
            k = i - 2
            core_copy(k).wait_recv()
            total = keep1[k] + in1[k].astype(jnp.float32)
            keep2[k] = jnp.where(y0 == 0, total[0], total[1])
            out2[k] = jnp.where(y0 == 0, total[1], total[0]).astype(jnp.bfloat16)
            row_copy(k).start()

        @pl.when((i >= 6) & (i < o_chunks + 6))
        def _():
            k = i - 6
            row_copy(k).wait_recv()
            total = keep2[k] + in2[k].astype(jnp.float32)
            total = total.reshape(at_count, tok_rows, O_COLS)
            out3[k] = total.astype(jnp.bfloat16)
            which = lax.broadcasted_iota(jnp.int32, total.shape, 0)
            keep3[k] = jnp.sum(jnp.where(which == a0, total, 0.0), axis=0)
            for j in range(1, at_count):
                col_copy(k, j).start()

        @pl.when(i >= 9)
        def _():
            k = i - 9
            for j in range(1, at_count):
                col_copy(k, j).wait_recv()
            total = keep3[k] + jnp.sum(in3[k].astype(jnp.float32), axis=0)
            o_ref[:, pl.ds(pl.multiple_of(k * O_COLS, O_COLS), O_COLS)] = total.astype(jnp.bfloat16)
            core_copy(k).wait_send()
            row_copy(k).wait_send()
            for j in range(1, at_count):
                col_copy(k, j).wait_send()

        return carry

    lax.fori_loop(0, o_chunks + 9, down, 0)
    for j in range(1, at_count):
        z_copy(j, own).wait_send()
    for j in range(at_count):
        y_copy(j, block(e0, j)).wait_send()
        c_copy(j, block(e0, j)).wait_send()
        c_copy(4 + j, block(e_y, j)).wait_send()


def fused_layers(
    tokens, expert_ids, gates, w_in, w_out, q_latent, q_rope, cache_latent, cache_rope, lengths
):
    tok_rows, model_width = tokens.shape
    slot_count, _, _, hid_units = w_in.shape
    rows = 16 * tok_rows
    chunks = model_width // O_COLS
    jbs = hid_units // LANES
    hit = expert_ids[:, :, None] == jnp.arange(LANES)[None, None, :]
    dense = jnp.sum(jnp.where(hit, gates[:, :, None], jnp.bfloat16(0)), axis=1)
    block = jnp.concatenate([tokens, dense.astype(jnp.bfloat16)], axis=1)
    rope_q = q_rope.reshape(q_latent.shape[0], q_latent.shape[1], -1)
    bf16, f32 = jnp.bfloat16, jnp.float32
    dma = pltpu.SemaphoreType.DMA
    return pl.pallas_call(
        moe_kernel,
        out_shape=(
            jax.ShapeDtypeStruct((tok_rows, model_width), bf16),
            jax.ShapeDtypeStruct(q_latent.shape, bf16),
        ),
        in_specs=[
            pl.BlockSpec(memory_space=pltpu.VMEM),
            pl.BlockSpec(memory_space=pl.ANY),
            pl.BlockSpec(memory_space=pl.ANY),
            pl.BlockSpec(memory_space=pltpu.VMEM),
            pl.BlockSpec(memory_space=pltpu.VMEM),
            pl.BlockSpec(memory_space=pltpu.VMEM),
            pl.BlockSpec(memory_space=pltpu.VMEM),
            pl.BlockSpec(memory_space=pltpu.SMEM),
        ],
        out_specs=(
            pl.BlockSpec(memory_space=pltpu.VMEM),
            pl.BlockSpec(memory_space=pltpu.VMEM),
        ),
        scratch_shapes=[
            pltpu.VMEM((16, tok_rows, model_width + LANES), bf16),
            pltpu.VMEM((2 * rows, 2 * model_width), bf16),
            pltpu.VMEM((W_SLOTS, jbs, 2 * D_BLOCK, LANES), bf16),
            pltpu.VMEM((O_SLOTS, slot_count, hid_units, O_COLS), bf16),
            pltpu.VMEM((2 * rows, hid_units), f32),
            pltpu.VMEM((rows, slot_count * hid_units), bf16),
            pltpu.VMEM((chunks, 2, rows // 4, O_COLS), f32),
            pltpu.VMEM((chunks, 2, rows // 4, O_COLS), bf16),
            pltpu.VMEM((chunks, 2, rows // 4, O_COLS), bf16),
            pltpu.VMEM((chunks, rows // 4, O_COLS), f32),
            pltpu.VMEM((chunks, rows // 4, O_COLS), bf16),
            pltpu.VMEM((chunks, rows // 4, O_COLS), bf16),
            pltpu.VMEM((chunks, tok_rows, O_COLS), f32),
            pltpu.VMEM((chunks, 4, tok_rows, O_COLS), bf16),
            pltpu.VMEM((chunks, 3, tok_rows, O_COLS), bf16),
            dma((W_SLOTS, jbs)), dma((O_SLOTS,)),
            dma((3,)), dma((3,)), dma((4,)), dma((4,)), dma((8,)), dma((8,)),
            dma((chunks,)), dma((chunks,)), dma((chunks,)), dma((chunks,)),
            dma((chunks, 3)), dma((chunks, 3)),
        ],
        compiler_params=pltpu.CompilerParams(
            collective_id=0, has_side_effects=True, vmem_limit_bytes=61 << 20
        ),
    )(block, w_in, w_out, q_latent, rope_q, cache_latent, cache_rope, lengths)


def expert_part(row_block, row_gates, w_in, w_out):
    slot_count, model_width, pair_count, hid_units = w_in.shape
    gate_up = jnp.einsum(
        "srd,sdf->srf",
        row_block,
        w_in.reshape(slot_count, model_width, pair_count * hid_units),
        preferred_element_type=jnp.float32,
    )
    hidden = (jax.nn.silu(gate_up[..., :hid_units]) * gate_up[..., hid_units:]).astype(jnp.bfloat16)
    down_out = jnp.einsum("srf,sfd->srd", hidden, w_out, preferred_element_type=jnp.float32)
    return (down_out * row_gates[..., None].astype(jnp.float32)).astype(jnp.bfloat16)


def latent_attention(q_latent, q_rope, cache_latent, cache_rope, lengths):
    att_rows, head_count, latent_width = q_latent.shape
    positions = cache_latent.shape[1]
    rope_q = q_rope.reshape(att_rows, head_count, -1)
    scores = jnp.einsum("ahl,acl->ahc", q_latent, cache_latent, preferred_element_type=jnp.float32)
    scores = scores + jnp.einsum(
        "ahr,arc->ahc", rope_q, cache_rope, preferred_element_type=jnp.float32
    )
    scores = scores * 192.0 ** (-0.5)
    visible = jnp.arange(positions)[None, None, :] < lengths[:, None, None]
    scores = jnp.where(visible, scores, -1e30)
    peak = jnp.max(scores, axis=2, keepdims=True)
    expo = jnp.where(visible, jnp.exp(scores - peak), 0.0)
    probs = (expo / jnp.sum(expo, axis=2, keepdims=True)).astype(jnp.bfloat16)
    context = jnp.einsum("ahc,acl->ahl", probs, cache_latent, preferred_element_type=jnp.float32)
    return context.astype(jnp.bfloat16)


def routed_experts(
    tokens, expert_ids, gates, w_in, w_out
):
    tok_rows, model_width = tokens.shape
    top_count = expert_ids.shape[1]
    slot_count = w_in.shape[0]
    ex_count = lax.axis_size("ex")
    at_count = lax.axis_size("at")
    experts = slot_count * ex_count
    slot_rows = experts * CAP
    flat_ids = expert_ids.reshape(-1)
    onehot = (flat_ids[:, None] == jnp.arange(experts)[None, :]).astype(jnp.int32)
    before = jnp.cumsum(onehot, axis=0) - onehot
    position = jnp.sum(before * onehot, axis=1)
    column = flat_ids // slot_count
    slot_index = flat_ids % slot_count
    target = (slot_index * ex_count + column) * CAP + position
    placed = target[None, :] == jnp.arange(slot_rows)[:, None]
    placed_rows = placed.reshape(slot_rows, tok_rows, top_count).any(axis=2).astype(jnp.bfloat16)
    packed = jnp.dot(placed_rows, tokens, preferred_element_type=jnp.float32).astype(jnp.bfloat16)
    packed = packed.reshape(slot_count, ex_count, CAP, model_width)
    packed_gates = jnp.dot(
        placed.astype(jnp.bfloat16), gates.reshape(-1), preferred_element_type=jnp.float32
    )
    packed_gates = packed_gates.astype(jnp.bfloat16).reshape(slot_count, ex_count, CAP)
    spread = jnp.broadcast_to(
        packed[:, :, None], (slot_count, ex_count, at_count, CAP, model_width)
    )
    spread = spread.reshape(slot_count, ex_count * at_count, CAP, model_width)
    spread_gates = jnp.broadcast_to(packed_gates[:, :, None], (slot_count, ex_count, at_count, CAP))
    spread_gates = spread_gates.reshape(slot_count, ex_count * at_count, CAP)
    arrived, arrived_gates = (
        lax.all_to_all(spread, ("ex", "at"), split_axis=1, concat_axis=1, tiled=True),
        lax.all_to_all(spread_gates, ("ex", "at"), split_axis=1, concat_axis=1, tiled=True),
    )
    partial_value = expert_part(
        arrived.reshape(slot_count, -1, model_width),
        arrived_gates.reshape(slot_count, -1),
        w_in,
        w_out,
    )
    partial_value = partial_value.reshape(slot_count, ex_count * at_count, CAP, model_width)
    returned = lax.all_to_all(partial_value, ("ex", "at"), split_axis=1, concat_axis=1, tiled=True)
    out_rows = jnp.sum(
        returned.reshape(slot_count, ex_count, at_count, CAP, model_width).astype(jnp.float32),
        axis=2,
    )
    flat_out = out_rows.reshape(slot_rows, model_width)
    moe_out = jnp.sum(flat_out[target.reshape(tok_rows, top_count)], axis=1).astype(jnp.bfloat16)
    return moe_out


def per_device(
    fused, tokens, expert_ids, gates, w_in, w_out, q_latent, q_rope, cache_latent, cache_rope, lengths
):
    if fused:
        return fused_layers(
            tokens, expert_ids, gates, w_in, w_out, q_latent, q_rope, cache_latent, cache_rope, lengths
        )
    moe_out = routed_experts(tokens, expert_ids, gates, w_in, w_out)
    context = latent_attention(q_latent, q_rope, cache_latent, cache_rope, lengths)
    return (moe_out, context)


def solution(mesh):
    fused = mesh.shape["ex"] == 4 and mesh.shape["at"] == 4
    return jax.shard_map(
        functools.partial(per_device, fused),
        mesh=mesh,
        in_specs=(
            P(("grp", "ex", "at"), None),
            P(("grp", "ex", "at"), None),
            P(("grp", "ex", "at"), None),
            P("ex", None, None, "at"),
            P("ex", "at", None),
            P(("grp", "ex", "at"), None, None),
            P(("grp", "ex", "at"), None),
            P(("grp", "ex", "at"), None, None),
            P(("grp", "ex", "at"), None, None),
            P(("grp", "ex", "at")),
        ),
        out_specs=(P(("grp", "ex", "at"), None), P(("grp", "ex", "at"), None, None)),
        check_vma=False,
    )
```
